32 devices in a mesh: groups: 2 (over y), hid: 8 (over z, x), row: 2 (over core).
Axes of the slice: x: 2, y: 2, z: 4, core: 2. Of those that a mesh axis runs over, the one named last changes fastest.
Arguments:
- iterate: bfloat16 [7168, 2560], P('hid', ('groups', 'row')), parts along dimension 1, may hold values from -0.06298828 to 0.06298828
Outputs:
- update: float32 [7168, 2560], P('hid', ('groups', 'row')), parts along dimension 1
The draws below stay inside these ranges and needn't reach their ends.
There are 2 independent parts, one for each index of `groups`. The reference program is written for one: setup_inputs(seed, part) draws one part's arguments, and reference() takes and returns one part's arrays. A program takes and returns all parts, laid end to end along the dimension named above; each array names one. Nothing has to cross between parts.
All inputs are finite; a program needn't handle non-finite values.
Results may differ from the reference program's by a relative error of at most 0.0007.
Values may be sent and summed in bfloat16 or wider, within the bound.
A program may use at most 64 MiB of HBM per device.

```python
import math
import jax
import jax.numpy as jnp

H = 7168
R = 1280


def with_spikes(result, own_key, source, target, parts, factor):
    def block_of(axis_at):
        return (jnp.arange(result.shape[axis_at]) // (result.shape[axis_at] // parts)).reshape((-1,) + (1,) * (result.ndim - 1 - axis_at))

    first = jax.random.permutation(own_key, parts)[block_of(target)]
    second = (block_of(target) + parts // 2) % parts
    return jnp.where((block_of(source) == first) | (block_of(source) == second), factor * result, result)


def level_of(stream_key, extent, pieces, least, top_value):
    def one(axis_at, shards_of):
        draws = jax.random.uniform(jax.random.fold_in(jax.random.fold_in(stream_key, 6), axis_at), (shards_of,), jnp.float32, least / len(pieces), top_value / len(pieces))
        return jnp.repeat(jnp.exp(draws), extent[axis_at] // shards_of).reshape((-1,) + (1,) * (len(extent) - axis_at - 1))

    gain = one(*pieces[0])
    for cut in pieces[1:]:
        gain = gain * one(*cut)
    return gain


def noise_with(rng, shape, scale, reach, split, heavy, held_as=jnp.bfloat16):
    entries = scale * jax.random.normal(rng, shape, jnp.float32)
    if split:
        entries = entries * level_of(rng, shape, split, -0.22, 0.18)
    return jnp.clip(with_spikes(entries, jax.random.fold_in(rng, 3), *heavy), -reach, reach).astype(held_as)


def setup_inputs(seed: int = 0, part: int = 0) -> dict:
    splits = jax.random.split(jax.random.key(seed), 2)
    own_keys = jax.random.split(jax.random.fold_in(splits[1], part), 2)
    iterate = noise_with(own_keys[0], (H, R), 0.01049, 0.06298828, ((0, 8), (1, 2)), (0, 1, 8, 2.0))
    return {"iterate": iterate}


coef_a = 3.4445
coef_b = -4.775
coef_c = 2.0315
update_scale = 0.2

def reference(iterate):
    gram_mat = jnp.dot(iterate.T, iterate, preferred_element_type=jnp.float32).astype(jnp.bfloat16)
    square = jnp.dot(gram_mat, gram_mat, preferred_element_type=jnp.float32)
    mixing = (coef_b * gram_mat.astype(jnp.float32) + coef_c * square).astype(jnp.bfloat16)
    product = jnp.dot(iterate, mixing, preferred_element_type=jnp.float32)
    return update_scale * math.sqrt(H) * (coef_a * iterate.astype(jnp.float32) + product)
```

```python
import math

import jax
import jax.numpy as jnp
from jax import lax
from jax.experimental import pallas as pl
from jax.experimental.pallas import tpu as pltpu
from jax.sharding import PartitionSpec as P

H = 7168


coef_a = 3.4445
coef_b = -4.775
coef_c = 2.0315
update_scale = 0.2

SUB = 128
X_CHIPS = 2
Z_CHIPS = 4


def swapped(shard, axis, bit):
    return lax.ppermute(shard, axis, [(i, i ^ 1 << bit) for i in range(lax.axis_size(axis))])


def body(iterate):
    half_rows = iterate.shape[1]
    full_rows = lax.all_gather(iterate, "row", axis=1, tiled=True)
    gram_tile = lax.psum_scatter(
        lax.dot_general(
            full_rows, iterate, (((0,), (0,)), ((), ())), preferred_element_type=jnp.float32
        ),
        "hid",
        scatter_dimension=0,
        tiled=True,
    ).astype(jnp.bfloat16)
    row_index = lax.axis_index("row")
    gram_cols = lax.all_gather(gram_tile, "hid", axis=0, tiled=True)
    partner_cols = swapped(gram_cols, "row", 0)
    own_rows = lax.dynamic_slice_in_dim(gram_cols, row_index * half_rows, half_rows, 0)
    other_rows = lax.dynamic_slice_in_dim(gram_cols, (1 - row_index) * half_rows, half_rows, 0)
    square = jnp.dot(gram_cols, own_rows, preferred_element_type=jnp.float32)
    square = square + jnp.dot(partner_cols, other_rows, preferred_element_type=jnp.float32)
    mixing = (coef_b * gram_cols.astype(jnp.float32) + coef_c * square).astype(jnp.bfloat16)
    product = jnp.dot(full_rows, mixing, preferred_element_type=jnp.float32)
    return update_scale * math.sqrt(H) * (coef_a * iterate.astype(jnp.float32) + product)


def aligned(value, unit=SUB):
    return pl.multiple_of(value, unit)


def kernel(
    strips, x_ref, out_ref, x_all, tiles, from_x, from_z, own_g, other_g, gram, mixing,
    x_send, x_recv, rs_x_send, rs_x_recv, rs_z_send, rs_z_recv,
    ag_z_send, ag_z_recv, ag_x_send, ag_x_recv, core_send, core_recv,
):
    rows, width = x_ref.shape
    blocks = 2 * strips
    depth = 3 * SUB
    half = depth // X_CHIPS
    piece = half // Z_CHIPS
    hid = lax.axis_index("hid")
    core = lax.axis_index("row")
    x, z = lax.rem(hid, X_CHIPS), lax.div(hid, X_CHIPS)
    x_peer = {"hid": hid + 1 - 2 * x}
    z_peers = [{"hid": lax.rem(z + d, Z_CHIPS) * X_CHIPS + x} for d in range(1, Z_CHIPS)]
    core_peer = {"row": 1 - core}

    barrier = pltpu.get_barrier_semaphore()
    for peer in [core_peer, x_peer, *z_peers]:
        pl.semaphore_signal(barrier, inc=1, device_id=peer, device_id_type=pl.DeviceIdType.MESH)
    pl.semaphore_wait(barrier, 2 + len(z_peers))

    def remote(src, dst, send, recv, peer):
        return pltpu.make_async_remote_copy(
            src_ref=src, dst_ref=dst, send_sem=send, recv_sem=recv,
            device_id=peer, device_id_type=pl.DeviceIdType.MESH,
        )

    own_cols = pl.ds(aligned(core * width), width)
    exchange = remote(x_ref, x_all.at[:, own_cols], x_send, x_recv, core_peer)
    exchange.start()
    x_all[:, own_cols] = x_ref[...]

    keep = pl.multiple_of(x * half, 16)
    give = pl.multiple_of((1 - x) * half, 16)
    mine = pl.multiple_of(x * half + z * piece, 16)

    def place(step, of_core):
        strip = lax.rem(step + 3 * of_core, strips)
        late = jnp.where(strip >= 3, 1, 0)
        lower = late + of_core - 2 * late * of_core
        return 2 * strip, 2 * strip + 3 * lower

    def rs_x(s):
        return remote(tiles.at[s, pl.ds(give, half)], from_x.at[s], rs_x_send.at[s], rs_x_recv.at[s], x_peer)

    def rs_z(s, d):
        there = lax.rem(z + d + 1, Z_CHIPS)
        src = tiles.at[s, pl.ds(pl.multiple_of(x * half + there * piece, 16), piece)]
        return remote(src, from_z.at[s, d], rs_z_send.at[s, d], rs_z_recv.at[s, d], z_peers[d])

    def ag_z(s, d):
        at = own_g.at[s, pl.ds(mine, piece)]
        return remote(at, at, ag_z_send.at[s, d], ag_z_recv.at[s, d], z_peers[d])

    def ag_x(s):
        at = own_g.at[s, pl.ds(keep, half)]
        return remote(at, at, ag_x_send.at[s], ag_x_recv.at[s], x_peer)

    def to_core(s):
        return remote(own_g.at[s], other_g.at[s], core_send.at[s], core_recv.at[s], core_peer)

    def first(s):
        if s == 1:
            exchange.wait()
            x_all[:, 2 * width :] = x_all[:, : 4 * SUB]
        col, row = place(s, core)
        tiles[s] = lax.dot_general(
            x_all[:, pl.ds(aligned(row * SUB), depth)],
            x_all[:, pl.ds(aligned(col * SUB), 2 * SUB)],
            (((0,), (0,)), ((), ())),
            preferred_element_type=jnp.float32,
        )
        rs_x(s).start()

    def after_rs_x(s):
        rs_x(s).wait()
        tiles[s, pl.ds(keep, half)] += from_x[s]
        for d in range(Z_CHIPS - 1):
            rs_z(s, d).start()

    def after_rs_z(s):
        for d in range(Z_CHIPS - 1):
            rs_z(s, d).wait()
        total = tiles[s, pl.ds(mine, piece)]
        for d in range(Z_CHIPS - 1):
            total += from_z[s, d]
        own_g[s, pl.ds(mine, piece)] = total.astype(jnp.bfloat16)
        for d in range(Z_CHIPS - 1):
            ag_z(s, d).start()

    def after_ag_z(s):
        for d in range(Z_CHIPS - 1):
            ag_z(s, d).wait()
        ag_x(s).start()

    def lay_out(s, held, of_core):
        col, row = place(s, of_core)
        for i in range(3):
            at = lax.rem(row + i, blocks)
            block = held[s, i * SUB : (i + 1) * SUB]
            gram[pl.ds(aligned(at * SUB), SUB), pl.ds(aligned(col * SUB), 2 * SUB)] = block
            gram[pl.ds(aligned(col * SUB), 2 * SUB), pl.ds(aligned(at * SUB), SUB)] = block.T

    def after_ag_x(s):
        ag_x(s).wait()
        to_core(s).start()
        lay_out(s, own_g, core)

    def last(s):
        to_core(s).wait()
        lay_out(s, other_g, 1 - core)

    stages = [first, after_rs_x, after_rs_z, after_ag_z, after_ag_x, last]
    for t in range(strips + len(stages) - 1):
        for at, stage in enumerate(stages):
            if 0 <= t - at < strips:
                stage(t - at)

    for i in range(strips):
        at = pl.ds(i * 2 * SUB, 2 * SUB)
        square = jnp.dot(gram[at], gram[:, own_cols], preferred_element_type=jnp.float32)
        mixing[at] = (coef_b * gram[at, own_cols].astype(jnp.float32) + coef_c * square).astype(jnp.bfloat16)
    step = 128
    for i in range(rows // step):
        at = pl.ds(i * step, step)
        product = jnp.dot(x_all[at, : 2 * width], mixing[...], preferred_element_type=jnp.float32)
        out_ref[at] = update_scale * math.sqrt(H) * (coef_a * x_ref[at].astype(jnp.float32) + product)


def fused(iterate):
    rows, width = iterate.shape
    full = 2 * width
    strips = full // (2 * SUB)
    depth = 3 * SUB
    half = depth // X_CHIPS
    piece = half // Z_CHIPS
    others = Z_CHIPS - 1
    dma = pltpu.SemaphoreType.DMA

    def run(*refs):
        kernel(strips, *refs)

    return pl.pallas_call(
        run,
        out_shape=jax.ShapeDtypeStruct((rows, width), jnp.float32),
        in_specs=[pl.BlockSpec(memory_space=pltpu.VMEM)],
        out_specs=pl.BlockSpec(memory_space=pltpu.VMEM),
        scratch_shapes=[
            pltpu.VMEM((rows, full + 4 * SUB), jnp.bfloat16),
            pltpu.VMEM((strips, depth, 2 * SUB), jnp.float32),
            pltpu.VMEM((strips, half, 2 * SUB), jnp.float32),
            pltpu.VMEM((strips, others, piece, 2 * SUB), jnp.float32),
            pltpu.VMEM((strips, depth, 2 * SUB), jnp.bfloat16),
            pltpu.VMEM((strips, depth, 2 * SUB), jnp.bfloat16),
            pltpu.VMEM((full, full), jnp.bfloat16),
            pltpu.VMEM((full, width), jnp.bfloat16),
            dma, dma,
            dma((strips,)), dma((strips,)),
            dma((strips, others)), dma((strips, others)),
            dma((strips, others)), dma((strips, others)),
            dma((strips,)), dma((strips,)),
            dma((strips,)), dma((strips,)),
        ],
        compiler_params=pltpu.CompilerParams(
            collective_id=0, has_side_effects=True, vmem_limit_bytes=48 * 1024 * 1024
        ),
        cost_estimate=pl.CostEstimate(
            flops=2 * (2 * rows + full) * full * width, bytes_accessed=6 * rows * width, transcendentals=0
        ),
    )(iterate)


def solution(mesh):
    fits = mesh.shape["hid"] == X_CHIPS * Z_CHIPS and mesh.shape["row"] == 2
    return jax.shard_map(
        fused if fits else body,
        mesh=mesh,
        in_specs=(P("hid", ("groups", "row")),),
        out_specs=P("hid", ("groups", "row")),
        check_vma=False,
    )
```

```python
import math

import jax
import jax.numpy as jnp
from jax import lax
from jax.experimental import pallas as pl
from jax.experimental.pallas import tpu as pltpu
from jax.sharding import PartitionSpec as P

H = 7168


coef_a = 3.4445
coef_b = -4.775
coef_c = 2.0315
update_scale = 0.2

SUB = 128
X_CHIPS = 2
Z_CHIPS = 4
CHUNKS = (
    (0, 0, 2, 0, 3, "xz"),
    (1, 0, 2, 0, 3, "nxf"),
    (2, 0, 2, 0, 3, "xfn"),
    (3, 0, 2, 0, 3, "nxf"),
    (4, 0, 1, 0, 3, "xnf"),
    (4, 1, 1, 0, 2, "xnf"),
    (4, 1, 1, 2, 1, "nxf"),
)
ORDER = (
    0, 1, 0, 2, 1, 3, 0, 2, 4, 1, 3, 5, 0, 4, 6, 3, 5, 4, 2, 6, 0, 1, 5, 0, 6, 3, 2, 4, 1, 5, 6, 2,
    3, 4, 1, 5, 6, 3, 4, 2, 6, 1, 5, 4, 1, 3, 4, 6, 2, 5, 3, 6, 2, 5,
)
WAYS = {"x": 2, "n": 2, "f": 2, "z": 4, "d": 8}


def swapped(shard, axis, bit):
    return lax.ppermute(shard, axis, [(i, i ^ 1 << bit) for i in range(lax.axis_size(axis))])


def body(iterate):
    half_rows = iterate.shape[1]
    full_rows = lax.all_gather(iterate, "row", axis=1, tiled=True)
    gram_tile = lax.psum_scatter(
        lax.dot_general(
            full_rows, iterate, (((0,), (0,)), ((), ())), preferred_element_type=jnp.float32
        ),
        "hid",
        scatter_dimension=0,
        tiled=True,
    ).astype(jnp.bfloat16)
    row_index = lax.axis_index("row")
    gram_cols = lax.all_gather(gram_tile, "hid", axis=0, tiled=True)
    partner_cols = swapped(gram_cols, "row", 0)
    own_rows = lax.dynamic_slice_in_dim(gram_cols, row_index * half_rows, half_rows, 0)
    other_rows = lax.dynamic_slice_in_dim(gram_cols, (1 - row_index) * half_rows, half_rows, 0)
    square = jnp.dot(gram_cols, own_rows, preferred_element_type=jnp.float32)
    square = square + jnp.dot(partner_cols, other_rows, preferred_element_type=jnp.float32)
    mixing = (coef_b * gram_cols.astype(jnp.float32) + coef_c * square).astype(jnp.bfloat16)
    product = jnp.dot(full_rows, mixing, preferred_element_type=jnp.float32)
    return update_scale * math.sqrt(H) * (coef_a * iterate.astype(jnp.float32) + product)


def aligned(value, unit=SUB):
    return pl.multiple_of(value, unit)


def stage_rows(stages, left):
    rows = []
    for kind in stages:
        left //= WAYS[kind]
        rows.append(left)
    return rows


def kernel(strips, x_ref, out_ref, x_all, gram, mixing, x_own, x_send, x_recv, x_sem, sends, recvs, *buffers):
    rows, width = x_ref.shape
    blocks = 2 * strips
    hid = lax.axis_index("hid")
    core = lax.axis_index("row")
    x, z = lax.rem(hid, X_CHIPS), lax.div(hid, X_CHIPS)
    near, far = lax.rem(z, 2), lax.div(z, 2)
    core_peer = {"row": 1 - core}
    place_in = {"x": x, "n": near, "f": far, "z": z, "d": hid}
    member = {
        "x": lambda p: z * X_CHIPS + p,
        "n": lambda p: (far * 2 + p) * X_CHIPS + x,
        "f": lambda p: (p * 2 + near) * X_CHIPS + x,
        "z": lambda p: p * X_CHIPS + x,
        "d": lambda p: p,
    }
    own_cols = pl.ds(aligned(core * width), width)
    fetch = pltpu.make_async_copy(x_ref, x_own, x_sem.at[0])
    fetch.start()

    kinds = set("".join(chunk[5] for chunk in CHUNKS))
    barrier = pltpu.get_barrier_semaphore()
    if "d" in kinds:
        greeted = [lax.rem(hid + d, 8) for d in range(1, 8)]
    else:
        greeted = [z * X_CHIPS + 1 - x] + [lax.rem(z + d, Z_CHIPS) * X_CHIPS + x for d in range(1, Z_CHIPS)]
    for peer in [core_peer] + [{"hid": one} for one in greeted]:
        pl.semaphore_signal(barrier, inc=1, device_id=peer, device_id_type=pl.DeviceIdType.MESH)
    pl.semaphore_wait(barrier, 1 + len(greeted))

    used = [0]

    def remote(src, dst, peer):
        at = used[0]
        used[0] += 1
        return pltpu.make_async_remote_copy(
            src_ref=src, dst_ref=dst, send_sem=sends.at[at], recv_sem=recvs.at[at],
            device_id=peer, device_id_type=pl.DeviceIdType.MESH,
        )

    exchange = pltpu.make_async_remote_copy(
        src_ref=x_ref, dst_ref=x_all.at[:, own_cols], send_sem=x_send, recv_sem=x_recv,
        device_id=core_peer, device_id_type=pl.DeviceIdType.MESH,
    )
    exchange.start()
    fetch.wait()
    x_all[:, own_cols] = x_own[...]

    def place(step, of_core):
        strip = lax.rem(step + 3 * of_core, strips)
        late = jnp.where(strip >= 3, 1, 0)
        lower = late + of_core - 2 * late * of_core
        return 2 * strip, 2 * strip + 3 * lower

    buffers = list(buffers)

    def add_chunk(order, step, first_block, n_blocks, first_row, n_rows, stages):
        depth = n_rows * SUB
        events = []
        tile, own_g, other_g = buffers.pop(0), buffers.pop(0), buffers.pop(0)
        arrive = [buffers.pop(0) for _ in stages]
        lefts = stage_rows(stages, depth)
        starts, at = [], 0
        for kind, left in zip(stages, lefts):
            starts.append(at)
            at = at + place_in[kind] * left

        def span(start, n):
            return pl.ds(pl.multiple_of(start, 16), n)

        def peers_of(kind):
            ways = WAYS[kind]
            return [lax.rem(place_in[kind] + d, ways) for d in range(1, ways)]

        sums, copies = [], []
        for i, kind in enumerate(stages):
            sums.append([
                remote(tile.at[span(starts[i] + p * lefts[i], lefts[i])], arrive[i].at[d], {"hid": member[kind](p)})
                for d, p in enumerate(peers_of(kind))
            ])
        for i in reversed(range(len(stages))):
            kind = stages[i]
            held = own_g.at[span(starts[i] + place_in[kind] * lefts[i], lefts[i])]
            copies.append([remote(held, held, {"hid": member[kind](p)}) for p in peers_of(kind)])
        copies.append([remote(own_g, other_g, core_peer)])

        def start(group):
            for one in group:
                one.start()

        def wait(group):
            for one in group:
                one.wait()

        def lay_out(held, of_core):
            col, row = place(step, of_core)
            for i in range(n_rows):
                at = lax.rem(row + first_row + i, blocks)
                block = held[i * SUB : (i + 1) * SUB]
                cols = pl.ds(aligned((col + first_block) * SUB), n_blocks * SUB)
                gram[pl.ds(aligned(at * SUB), SUB), cols] = block
                gram[cols, pl.ds(aligned(at * SUB), SUB)] = block.T

        def first():
            if order == second:
                exchange.wait()
                x_all[:, 2 * width :] = x_all[:, : 4 * SUB]
            col, row = place(step, core)
            tile[...] = lax.dot_general(
                x_all[:, pl.ds(aligned((row + first_row) * SUB), depth)],
                x_all[:, pl.ds(aligned((col + first_block) * SUB), n_blocks * SUB)],
                (((0,), (0,)), ((), ())),
                preferred_element_type=jnp.float32,
            )
            start(sums[0])

        def after_sum(i):
            wait(sums[i])
            kind, left = stages[i], lefts[i]
            kept = span(starts[i] + place_in[kind] * left, left)
            total = tile[kept]
            for d in range(WAYS[kind] - 1):
                total += arrive[i][d]
            if i + 1 < len(stages):
                tile[kept] = total
                start(sums[i + 1])
            else:
                own_g[kept] = total.astype(jnp.bfloat16)
                start(copies[0])

        def after_copy(i):
            wait(copies[i])
            if i + 1 < len(copies):
                start(copies[i + 1])
            if i + 2 == len(copies):
                lay_out(own_g, core)
            if i + 1 == len(copies):
                lay_out(other_g, 1 - core)

        events.append((first, ()))
        for i in range(len(stages)):
            events.append((after_sum, (i,)))
        for i in range(len(copies)):
            events.append((after_copy, (i,)))
        return events

    second = min(i for i, chunk in enumerate(CHUNKS) if chunk[0] > 0)
    todo = [add_chunk(order, *chunk) for order, chunk in enumerate(CHUNKS)]
    for chunk in ORDER:
        run, at = todo[chunk].pop(0)
        run(*at)

    for i in range(strips):
        at = pl.ds(i * 2 * SUB, 2 * SUB)
        square = jnp.dot(gram[at], gram[:, own_cols], preferred_element_type=jnp.float32)
        mixing[at] = (coef_b * gram[at, own_cols].astype(jnp.float32) + coef_c * square).astype(jnp.bfloat16)
    step = 128
    for i in range(rows // step):
        at = pl.ds(i * step, step)
        product = jnp.dot(x_all[at, : 2 * width], mixing[...], preferred_element_type=jnp.float32)
        out_ref[at] = update_scale * math.sqrt(H) * (coef_a * x_own[at].astype(jnp.float32) + product)


def fused(iterate):
    rows, width = iterate.shape
    full = 2 * width
    strips = full // (2 * SUB)
    buffers, copies = [], 0
    for _, _, n_blocks, _, n_rows, stages in CHUNKS:
        cols, depth = n_blocks * SUB, n_rows * SUB
        buffers += [pltpu.VMEM((depth, cols), jnp.float32)] + [pltpu.VMEM((depth, cols), jnp.bfloat16)] * 2
        for kind, left in zip(stages, stage_rows(stages, depth)):
            buffers.append(pltpu.VMEM((WAYS[kind] - 1, left, cols), jnp.float32))
            copies += 2 * (WAYS[kind] - 1)
        copies += 1
    dma = pltpu.SemaphoreType.DMA

    def run(*refs):
        kernel(strips, *refs)

    return pl.pallas_call(
        run,
        out_shape=jax.ShapeDtypeStruct((rows, width), jnp.float32),
        in_specs=[pl.BlockSpec(memory_space=pl.ANY)],
        out_specs=pl.BlockSpec(memory_space=pltpu.VMEM),
        scratch_shapes=[
            pltpu.VMEM((rows, full + 4 * SUB), jnp.bfloat16),
            pltpu.VMEM((full, full), jnp.bfloat16),
            pltpu.VMEM((full, width), jnp.bfloat16),
            pltpu.VMEM((rows, width), jnp.bfloat16),
            dma, dma, dma((1,)),
            dma((copies,)), dma((copies,)),
            *buffers,
        ],
        compiler_params=pltpu.CompilerParams(
            collective_id=0, has_side_effects=True, vmem_limit_bytes=48 * 1024 * 1024
        ),
        cost_estimate=pl.CostEstimate(
            flops=2 * (2 * rows + full) * full * width, bytes_accessed=6 * rows * width, transcendentals=0
        ),
    )(iterate)


def solution(mesh):
    fits = mesh.shape["hid"] == X_CHIPS * Z_CHIPS and mesh.shape["row"] == 2
    return jax.shard_map(
        fused if fits else body,
        mesh=mesh,
        in_specs=(P("hid", ("groups", "row")),),
        out_specs=P("hid", ("groups", "row")),
        check_vma=False,
    )
```

```python
import math

import jax
import jax.numpy as jnp
from jax import lax
from jax.experimental import pallas as pl
from jax.experimental.pallas import tpu as pltpu
from jax.sharding import PartitionSpec as P

H = 7168


coef_a = 3.4445
coef_b = -4.775
coef_c = 2.0315
update_scale = 0.2

SUB = 128
X_CHIPS = 2
Z_CHIPS = 4
CHUNKS = (
    (0, 0, 2, 0, 3, "xnf"),
    (1, 0, 2, 0, 3, "nxf"),
    (2, 0, 2, 0, 3, "fxn"),
    (3, 0, 2, 0, 3, "xfn"),
    (4, 0, 2, 0, 3, "xnf"),
)
ORDER = (
    0, 1, 2, 3, 4, 0, 1, 3, 4, 0, 2, 1, 3, 4, 2, 0, 1, 3, 2, 4, 0, 3, 1, 2, 4, 0, 1, 3, 2, 4, 0, 1,
    0, 3, 1, 3, 4, 2, 4, 2,
)
WAYS = {"x": 2, "n": 2, "f": 2, "z": 4, "d": 8}


def swapped(shard, axis, bit):
    return lax.ppermute(shard, axis, [(i, i ^ 1 << bit) for i in range(lax.axis_size(axis))])


def body(iterate):
    half_rows = iterate.shape[1]
    full_rows = lax.all_gather(iterate, "row", axis=1, tiled=True)
    gram_tile = lax.psum_scatter(
        lax.dot_general(
            full_rows, iterate, (((0,), (0,)), ((), ())), preferred_element_type=jnp.float32
        ),
        "hid",
        scatter_dimension=0,
        tiled=True,
    ).astype(jnp.bfloat16)
    row_index = lax.axis_index("row")
    gram_cols = lax.all_gather(gram_tile, "hid", axis=0, tiled=True)
    partner_cols = swapped(gram_cols, "row", 0)
    own_rows = lax.dynamic_slice_in_dim(gram_cols, row_index * half_rows, half_rows, 0)
    other_rows = lax.dynamic_slice_in_dim(gram_cols, (1 - row_index) * half_rows, half_rows, 0)
    square = jnp.dot(gram_cols, own_rows, preferred_element_type=jnp.float32)
    square = square + jnp.dot(partner_cols, other_rows, preferred_element_type=jnp.float32)
    mixing = (coef_b * gram_cols.astype(jnp.float32) + coef_c * square).astype(jnp.bfloat16)
    product = jnp.dot(full_rows, mixing, preferred_element_type=jnp.float32)
    return update_scale * math.sqrt(H) * (coef_a * iterate.astype(jnp.float32) + product)


def aligned(value, unit=SUB):
    return pl.multiple_of(value, unit)


def stage_rows(stages, left):
    rows = []
    for kind in stages:
        left //= WAYS[kind]
        rows.append(left)
    return rows


def kernel(strips, x_ref, out_ref, x_all, gram, mixing, x_own, x_send, x_recv, x_sem, sends, recvs, *buffers):
    rows, width = x_ref.shape
    blocks = 2 * strips
    hid = lax.axis_index("hid")
    core = lax.axis_index("row")
    x, z = lax.rem(hid, X_CHIPS), lax.div(hid, X_CHIPS)
    near, far = lax.rem(z, 2), lax.div(z, 2)
    core_peer = {"row": 1 - core}
    place_in = {"x": x, "n": near, "f": far, "z": z, "d": hid}
    member = {
        "x": lambda p: z * X_CHIPS + p,
        "n": lambda p: (far * 2 + p) * X_CHIPS + x,
        "f": lambda p: (p * 2 + near) * X_CHIPS + x,
        "z": lambda p: p * X_CHIPS + x,
        "d": lambda p: p,
    }
    own_cols = pl.ds(aligned(core * width), width)
    fetch = pltpu.make_async_copy(x_ref, x_own, x_sem.at[0])
    fetch.start()

    kinds = set("".join(chunk[5] for chunk in CHUNKS))
    barrier = pltpu.get_barrier_semaphore()
    if "d" in kinds:
        greeted = [lax.rem(hid + d, 8) for d in range(1, 8)]
    else:
        greeted = [z * X_CHIPS + 1 - x] + [lax.rem(z + d, Z_CHIPS) * X_CHIPS + x for d in range(1, Z_CHIPS)]
    for peer in [core_peer] + [{"hid": one} for one in greeted]:
        pl.semaphore_signal(barrier, inc=1, device_id=peer, device_id_type=pl.DeviceIdType.MESH)
    pl.semaphore_wait(barrier, 1 + len(greeted))

    used = [0]

    def remote(src, dst, peer):
        at = used[0]
        used[0] += 1
        return pltpu.make_async_remote_copy(
            src_ref=src, dst_ref=dst, send_sem=sends.at[at], recv_sem=recvs.at[at],
            device_id=peer, device_id_type=pl.DeviceIdType.MESH,
        )

    exchange = pltpu.make_async_remote_copy(
        src_ref=x_ref, dst_ref=x_all.at[:, own_cols], send_sem=x_send, recv_sem=x_recv,
        device_id=core_peer, device_id_type=pl.DeviceIdType.MESH,
    )
    exchange.start()
    fetch.wait()
    x_all[:, own_cols] = x_own[...]

    def place(step, of_core):
        strip = lax.rem(step + 3 * of_core, strips)
        late = jnp.where(strip >= 3, 1, 0)
        lower = late + of_core - 2 * late * of_core
        return 2 * strip, 2 * strip + 3 * lower

    buffers = list(buffers)

    def add_chunk(order, step, first_block, n_blocks, first_row, n_rows, stages):
        depth = n_rows * SUB
        events = []
        tile, own_g, other_g = buffers.pop(0), buffers.pop(0), buffers.pop(0)
        arrive = [buffers.pop(0) for _ in stages]
        lefts = stage_rows(stages, depth)
        starts, at = [], 0
        for kind, left in zip(stages, lefts):
            starts.append(at)
            at = at + place_in[kind] * left

        def span(start, n):
            return pl.ds(pl.multiple_of(start, 16), n)

        def peers_of(kind):
            ways = WAYS[kind]
            return [lax.rem(place_in[kind] + d, ways) for d in range(1, ways)]

        sums, copies = [], []
        for i, kind in enumerate(stages):
            sums.append([
                remote(tile.at[span(starts[i] + p * lefts[i], lefts[i])], arrive[i].at[d], {"hid": member[kind](p)})
                for d, p in enumerate(peers_of(kind))
            ])
        for i in reversed(range(len(stages))):
            kind = stages[i]
            held = own_g.at[span(starts[i] + place_in[kind] * lefts[i], lefts[i])]
            copies.append([remote(held, held, {"hid": member[kind](p)}) for p in peers_of(kind)])
        copies.append([remote(own_g, other_g, core_peer)])

        def start(group):
            for one in group:
                one.start()

        def wait(group):
            for one in group:
                one.wait()

        def lay_out(held, of_core):
            col, row = place(step, of_core)
            for i in range(n_rows):
                at = lax.rem(row + first_row + i, blocks)
                block = held[i * SUB : (i + 1) * SUB]
                cols = pl.ds(aligned((col + first_block) * SUB), n_blocks * SUB)
                gram[pl.ds(aligned(at * SUB), SUB), cols] = block
                gram[cols, pl.ds(aligned(at * SUB), SUB)] = block.T

        def first():
            if order == second:
                exchange.wait()
                x_all[:, 2 * width :] = x_all[:, : 4 * SUB]
            col, row = place(step, core)
            tile[...] = lax.dot_general(
                x_all[:, pl.ds(aligned((row + first_row) * SUB), depth)],
                x_all[:, pl.ds(aligned((col + first_block) * SUB), n_blocks * SUB)],
                (((0,), (0,)), ((), ())),
                preferred_element_type=jnp.float32,
            )
            start(sums[0])

        def after_sum(i):
            wait(sums[i])
            kind, left = stages[i], lefts[i]
            kept = span(starts[i] + place_in[kind] * left, left)
            total = tile[kept]
            for d in range(WAYS[kind] - 1):
                total += arrive[i][d]
            if i + 1 < len(stages):
                tile[kept] = total
                start(sums[i + 1])
            else:
                own_g[kept] = total.astype(jnp.bfloat16)
                start(copies[0])

        def after_copy(i):
            wait(copies[i])
            if i + 1 < len(copies):
                start(copies[i + 1])
            if i + 2 == len(copies):
                lay_out(own_g, core)
            if i + 1 == len(copies):
                lay_out(other_g, 1 - core)

        events.append((first, ()))
        for i in range(len(stages)):
            events.append((after_sum, (i,)))
        for i in range(len(copies)):
            events.append((after_copy, (i,)))
        return events

    second = min(i for i, chunk in enumerate(CHUNKS) if chunk[0] > 0)
    todo = [add_chunk(order, *chunk) for order, chunk in enumerate(CHUNKS)]
    for chunk in ORDER:
        run, at = todo[chunk].pop(0)
        run(*at)

    full = 2 * width
    step = full // 2
    for i in range(full // step):
        at = pl.ds(i * step, step)
        square = jnp.dot(gram[at], gram[:, own_cols], preferred_element_type=jnp.float32)
        mixing[at] = (coef_b * gram[at, own_cols].astype(jnp.float32) + coef_c * square).astype(jnp.bfloat16)
    step = rows // 2
    for i in range(rows // step):
        at = pl.ds(i * step, step)
        product = jnp.dot(x_all[at, :full], mixing[...], preferred_element_type=jnp.float32)
        out_ref[at] = update_scale * math.sqrt(H) * (coef_a * x_own[at].astype(jnp.float32) + product)


def fused(iterate):
    rows, width = iterate.shape
    full = 2 * width
    strips = full // (2 * SUB)
    buffers, copies = [], 0
    for _, _, n_blocks, _, n_rows, stages in CHUNKS:
        cols, depth = n_blocks * SUB, n_rows * SUB
        buffers += [pltpu.VMEM((depth, cols), jnp.float32)] + [pltpu.VMEM((depth, cols), jnp.bfloat16)] * 2
        for kind, left in zip(stages, stage_rows(stages, depth)):
            buffers.append(pltpu.VMEM((WAYS[kind] - 1, left, cols), jnp.float32))
            copies += 2 * (WAYS[kind] - 1)
        copies += 1
    dma = pltpu.SemaphoreType.DMA

    def run(*refs):
        kernel(strips, *refs)

    return pl.pallas_call(
        run,
        out_shape=jax.ShapeDtypeStruct((rows, width), jnp.float32),
        in_specs=[pl.BlockSpec(memory_space=pl.ANY)],
        out_specs=pl.BlockSpec(memory_space=pltpu.VMEM),
        scratch_shapes=[
            pltpu.VMEM((rows, full + 4 * SUB), jnp.bfloat16),
            pltpu.VMEM((full, full), jnp.bfloat16),
            pltpu.VMEM((full, width), jnp.bfloat16),
            pltpu.VMEM((rows, width), jnp.bfloat16),
            dma, dma, dma((1,)),
            dma((copies,)), dma((copies,)),
            *buffers,
        ],
        compiler_params=pltpu.CompilerParams(
            collective_id=0, has_side_effects=True, vmem_limit_bytes=48 * 1024 * 1024
        ),
        cost_estimate=pl.CostEstimate(
            flops=2 * (2 * rows + full) * full * width, bytes_accessed=6 * rows * width, transcendentals=0
        ),
    )(iterate)


def solution(mesh):
    fits = mesh.shape["hid"] == X_CHIPS * Z_CHIPS and mesh.shape["row"] == 2
    return jax.shard_map(
        fused if fits else body,
        mesh=mesh,
        in_specs=(P("hid", ("groups", "row")),),
        out_specs=P("hid", ("groups", "row")),
        check_vma=False,
    )
```

```python
import math

import jax
import jax.numpy as jnp
from jax import lax
from jax.experimental import pallas as pl
from jax.experimental.pallas import tpu as pltpu
from jax.sharding import PartitionSpec as P

H = 7168


coef_a = 3.4445
coef_b = -4.775
coef_c = 2.0315
update_scale = 0.2

SUB = 128
X_CHIPS = 2
Z_CHIPS = 4
CHUNKS = (
    (0, 0, 2, 0, 3, "xnf"),
    (1, 0, 2, 0, 3, "nxf"),
    (2, 0, 2, 0, 3, "fxn"),
    (3, 0, 2, 0, 3, "xfn"),
    (4, 0, 2, 0, 3, "xnf"),
)
ORDER = (
    0, 1, 2, 3, 4, 0, 1, 3, 4, 0, 2, 1, 3, 4, 2, 0, 1, 3, 2, 4, 0, 3, 1, 2, 4, 0, 1, 3, 2, 4, 0, 1,
    0, 3, 1, 3, 4, 2, 4, 2,
)
WAYS = {"x": 2, "n": 2, "f": 2, "z": 4, "d": 8}


def swapped(shard, axis, bit):
    return lax.ppermute(shard, axis, [(i, i ^ 1 << bit) for i in range(lax.axis_size(axis))])


def body(iterate):
    half_rows = iterate.shape[1]
    full_rows = lax.all_gather(iterate, "row", axis=1, tiled=True)
    gram_tile = lax.psum_scatter(
        lax.dot_general(
            full_rows, iterate, (((0,), (0,)), ((), ())), preferred_element_type=jnp.float32
        ),
        "hid",
        scatter_dimension=0,
        tiled=True,
    ).astype(jnp.bfloat16)
    row_index = lax.axis_index("row")
    gram_cols = lax.all_gather(gram_tile, "hid", axis=0, tiled=True)
    partner_cols = swapped(gram_cols, "row", 0)
    own_rows = lax.dynamic_slice_in_dim(gram_cols, row_index * half_rows, half_rows, 0)
    other_rows = lax.dynamic_slice_in_dim(gram_cols, (1 - row_index) * half_rows, half_rows, 0)
    square = jnp.dot(gram_cols, own_rows, preferred_element_type=jnp.float32)
    square = square + jnp.dot(partner_cols, other_rows, preferred_element_type=jnp.float32)
    mixing = (coef_b * gram_cols.astype(jnp.float32) + coef_c * square).astype(jnp.bfloat16)
    product = jnp.dot(full_rows, mixing, preferred_element_type=jnp.float32)
    return update_scale * math.sqrt(H) * (coef_a * iterate.astype(jnp.float32) + product)


def aligned(value, unit=SUB):
    return pl.multiple_of(value, unit)


def stage_rows(stages, left):
    rows = []
    for kind in stages:
        left //= WAYS[kind]
        rows.append(left)
    return rows


def kernel(strips, x_ref, out_ref, x_all, gram, mixing, x_own, x_send, x_recv, x_sem, sends, recvs, *buffers):
    rows, width = x_ref.shape
    blocks = 2 * strips
    hid = lax.axis_index("hid")
    core = lax.axis_index("row")
    x, z = lax.rem(hid, X_CHIPS), lax.div(hid, X_CHIPS)
    near, far = lax.rem(z, 2), lax.div(z, 2)
    core_peer = {"row": 1 - core}
    place_in = {"x": x, "n": near, "f": far, "z": z, "d": hid}
    member = {
        "x": lambda p: z * X_CHIPS + p,
        "n": lambda p: (far * 2 + p) * X_CHIPS + x,
        "f": lambda p: (p * 2 + near) * X_CHIPS + x,
        "z": lambda p: p * X_CHIPS + x,
        "d": lambda p: p,
    }
    own_cols = pl.ds(aligned(core * width), width)
    fetch = pltpu.make_async_copy(x_ref, x_own, x_sem.at[0])
    fetch.start()

    kinds = set("".join(chunk[5] for chunk in CHUNKS))
    barrier = pltpu.get_barrier_semaphore()
    if "d" in kinds:
        greeted = [lax.rem(hid + d, 8) for d in range(1, 8)]
    else:
        greeted = [z * X_CHIPS + 1 - x] + [lax.rem(z + d, Z_CHIPS) * X_CHIPS + x for d in range(1, Z_CHIPS)]
    for peer in [core_peer] + [{"hid": one} for one in greeted]:
        pl.semaphore_signal(barrier, inc=1, device_id=peer, device_id_type=pl.DeviceIdType.MESH)
    pl.semaphore_wait(barrier, 1 + len(greeted))

    used = [0]

    def remote(src, dst, peer):
        at = used[0]
        used[0] += 1
        return pltpu.make_async_remote_copy(
            src_ref=src, dst_ref=dst, send_sem=sends.at[at], recv_sem=recvs.at[at],
            device_id=peer, device_id_type=pl.DeviceIdType.MESH,
        )

    exchange = pltpu.make_async_remote_copy(
        src_ref=x_ref, dst_ref=x_all.at[:, own_cols], send_sem=x_send, recv_sem=x_recv,
        device_id=core_peer, device_id_type=pl.DeviceIdType.MESH,
    )
    exchange.start()
    fetch.wait()
    x_all[:, own_cols] = x_own[...]

    def place(step, of_core):
        strip = lax.rem(step + 3 * of_core, strips)
        late = jnp.where(strip >= 3, 1, 0)
        lower = late + of_core - 2 * late * of_core
        return 2 * strip, 2 * strip + 3 * lower

    buffers = list(buffers)

    def add_chunk(order, step, first_block, n_blocks, first_row, n_rows, stages):
        depth = n_rows * SUB
        events = []
        tile, own_g, other_g = buffers.pop(0), buffers.pop(0), buffers.pop(0)
        arrive = [buffers.pop(0) for _ in stages]
        lefts = stage_rows(stages, depth)
        starts, at = [], 0
        for kind, left in zip(stages, lefts):
            starts.append(at)
            at = at + place_in[kind] * left

        def span(start, n):
            return pl.ds(pl.multiple_of(start, 16), n)

        def peers_of(kind):
            ways = WAYS[kind]
            return [lax.rem(place_in[kind] + d, ways) for d in range(1, ways)]

        sums, copies = [], []
        for i, kind in enumerate(stages):
            sums.append([
                remote(tile.at[span(starts[i] + p * lefts[i], lefts[i])], arrive[i].at[d], {"hid": member[kind](p)})
                for d, p in enumerate(peers_of(kind))
            ])
        for i in reversed(range(len(stages))):
            kind = stages[i]
            held = own_g.at[span(starts[i] + place_in[kind] * lefts[i], lefts[i])]
            copies.append([remote(held, held, {"hid": member[kind](p)}) for p in peers_of(kind)])
        copies.append([remote(own_g, other_g, core_peer)])

        def start(group):
            for one in group:
                one.start()

        def wait(group):
            for one in group:
                one.wait()

        def lay_out(held, of_core):
            col, row = place(step, of_core)
            for i in range(n_rows):
                at = lax.rem(row + first_row + i, blocks)
                block = held[i * SUB : (i + 1) * SUB]
                cols = pl.ds(aligned((col + first_block) * SUB), n_blocks * SUB)
                gram[pl.ds(aligned(at * SUB), SUB), cols] = block
                gram[cols, pl.ds(aligned(at * SUB), SUB)] = block.T

        def first():
            if order == second:
                exchange.wait()
                x_all[:, 2 * width :] = x_all[:, : 4 * SUB]
            col, row = place(step, core)
            tile[...] = lax.dot_general(
                x_all[:, pl.ds(aligned((row + first_row) * SUB), depth)],
                x_all[:, pl.ds(aligned((col + first_block) * SUB), n_blocks * SUB)],
                (((0,), (0,)), ((), ())),
                preferred_element_type=jnp.float32,
            )
            start(sums[0])

        def after_sum(i):
            wait(sums[i])
            kind, left = stages[i], lefts[i]
            kept = span(starts[i] + place_in[kind] * left, left)
            total = tile[kept]
            for d in range(WAYS[kind] - 1):
                total += arrive[i][d]
            if i + 1 < len(stages):
                tile[kept] = total
                start(sums[i + 1])
            else:
                own_g[kept] = total.astype(jnp.bfloat16)
                start(copies[0])

        def after_copy(i):
            wait(copies[i])
            if i + 1 < len(copies):
                start(copies[i + 1])
            if i + 2 == len(copies):
                lay_out(own_g, core)
            if i + 1 == len(copies):
                lay_out(other_g, 1 - core)

        events.append((first, ()))
        for i in range(len(stages)):
            events.append((after_sum, (i,)))
        for i in range(len(copies)):
            events.append((after_copy, (i,)))
        return events

    second = min(i for i, chunk in enumerate(CHUNKS) if chunk[0] > 0)
    todo = [add_chunk(order, *chunk) for order, chunk in enumerate(CHUNKS)]
    for chunk in ORDER:
        run, at = todo[chunk].pop(0)
        run(*at)

    full = 2 * width
    step = full
    for i in range(full // step):
        at = pl.ds(i * step, step)
        square = jnp.dot(gram[at], gram[:, own_cols], preferred_element_type=jnp.float32)
        mixing[at] = (coef_b * gram[at, own_cols].astype(jnp.float32) + coef_c * square).astype(jnp.bfloat16)
    step = rows
    for i in range(rows // step):
        at = pl.ds(i * step, step)
        product = jnp.dot(x_all[at, :full], mixing[...], preferred_element_type=jnp.float32)
        out_ref[at] = update_scale * math.sqrt(H) * (coef_a * x_own[at].astype(jnp.float32) + product)


def fused(iterate):
    rows, width = iterate.shape
    full = 2 * width
    strips = full // (2 * SUB)
    buffers, copies = [], 0
    for _, _, n_blocks, _, n_rows, stages in CHUNKS:
        cols, depth = n_blocks * SUB, n_rows * SUB
        buffers += [pltpu.VMEM((depth, cols), jnp.float32)] + [pltpu.VMEM((depth, cols), jnp.bfloat16)] * 2
        for kind, left in zip(stages, stage_rows(stages, depth)):
            buffers.append(pltpu.VMEM((WAYS[kind] - 1, left, cols), jnp.float32))
            copies += 2 * (WAYS[kind] - 1)
        copies += 1
    dma = pltpu.SemaphoreType.DMA

    def run(*refs):
        kernel(strips, *refs)

    return pl.pallas_call(
        run,
        out_shape=jax.ShapeDtypeStruct((rows, width), jnp.float32),
        in_specs=[pl.BlockSpec(memory_space=pl.ANY)],
        out_specs=pl.BlockSpec(memory_space=pltpu.VMEM),
        scratch_shapes=[
            pltpu.VMEM((rows, full + 4 * SUB), jnp.bfloat16),
            pltpu.VMEM((full, full), jnp.bfloat16),
            pltpu.VMEM((full, width), jnp.bfloat16),
            pltpu.VMEM((rows, width), jnp.bfloat16),
            dma, dma, dma((1,)),
            dma((copies,)), dma((copies,)),
            *buffers,
        ],
        compiler_params=pltpu.CompilerParams(
            collective_id=0, has_side_effects=True, vmem_limit_bytes=48 * 1024 * 1024
        ),
        cost_estimate=pl.CostEstimate(
            flops=2 * (2 * rows + full) * full * width, bytes_accessed=6 * rows * width, transcendentals=0
        ),
    )(iterate)


def solution(mesh):
    fits = mesh.shape["hid"] == X_CHIPS * Z_CHIPS and mesh.shape["row"] == 2
    return jax.shard_map(
        fused if fits else body,
        mesh=mesh,
        in_specs=(P("hid", ("groups", "row")),),
        out_specs=P("hid", ("groups", "row")),
        check_vma=False,
    )
```
